32 devices in a mesh: grp: 2 (over y), row: 4 (over x, core), col: 4 (over z).
Axes of the slice: x: 2, y: 2, z: 4, core: 2. Of those that a mesh axis runs over, the one named last changes fastest.
Arguments:
- left_factors: bfloat16 [8, 48, 32, 128], P(('grp', 'row'), 'col'), parts along dimension 0, may hold values from -6 to 6
- right_factors: bfloat16 [8, 48, 32, 128], P(('grp', 'col'), 'row'), parts along dimension 0, may hold values from -6 to 6
- out_weight: bfloat16 [1024, 128], replicated, may hold values from -2 to 2
- out_bias: float32 [128], replicated, may hold values from -4 to 4
- pair_grad: bfloat16 [384, 192, 128], P(('grp', 'row'), 'col'), parts along dimension 0, may hold values from -6 to 6
Outputs:
- pair_update: bfloat16 [384, 192, 128], P(('grp', 'row'), 'col'), parts along dimension 0
- grad_left: float32 [8, 48, 32, 128], P(('grp', 'row'), 'col'), parts along dimension 0
- grad_right: float32 [8, 48, 32, 128], P(('grp', 'col'), 'row'), parts along dimension 0
- grad_weight: float32 [2048, 128], P('grp'), parts along dimension 0
The draws below stay inside these ranges and needn't reach their ends.
There are 2 independent parts, one for each index of `grp`. The reference program is written for one: setup_inputs(seed, part) draws one part's arguments, and reference() takes and returns one part's arrays. A program takes and returns all parts, laid end to end along the dimension named above; an argument that names none is the same for every part. Nothing has to cross between parts.
All inputs are finite; a program needn't handle non-finite values.
Results may differ from the reference program's by a relative error of at most 0.004.
Values may be sent and summed in bfloat16 or wider, within the bound.
No kernel may reach another device: no remote copies, remote signals or barrier semaphores. Data moves between devices by JAX's collectives and lax.ppermute only.
A program may use at most 64 MiB of HBM per device.

```python
import jax
import jax.numpy as jnp
from jax import lax

CH = 32
H = 128
S = 128
RES_DEV = 48
K = 1024
L = 192
N_ROW = 4
N_COL = 4


def steps_of(own_key, dims, pieces, low, largest):
    factor_of = 1.0
    for axis_at, shards_of in pieces:
        steps = jax.random.uniform(jax.random.fold_in(jax.random.fold_in(own_key, 6), axis_at), (shards_of,), jnp.float32, low / len(pieces), largest / len(pieces))
        factor_of = factor_of * jnp.repeat(jnp.exp(steps), dims[axis_at] // shards_of).reshape((-1,) + (1,) * (len(dims) - 1 - axis_at))
    return factor_of


def gaussian(stream_key, shape, scale, most, cuts=(), held_as=jnp.bfloat16):
    entries = jax.random.normal(stream_key, shape, jnp.float32) * scale
    if len(cuts) > 0:
        entries = steps_of(stream_key, shape, cuts, -0.22, 0.18) * entries
    return jnp.clip(entries, min=-most, max=most).astype(held_as)


def setup_inputs(seed: int = 0, part: int = 0) -> dict:
    key_of = jax.random.split(jax.random.key(seed), 6)
    own_keys = jax.random.split(jax.random.fold_in(key_of[5], part), 6)
    return {
        "left_factors": gaussian(own_keys[0], (N_ROW, RES_DEV, CH, S), 1.0, 6.0, ((0, 4), (1, 4))),
        "right_factors": gaussian(own_keys[1], (N_COL, RES_DEV, CH, S), 1.0, 6.0, ((0, 4), (1, 4))),
        "out_weight": gaussian(key_of[2], (K, H), (CH * CH // S) ** -0.5, 2.0),
        "out_bias": gaussian(key_of[3], (H,), 1.0, 4.0, (), jnp.float32),
        "pair_grad": gaussian(own_keys[4], (L, L, H), 1.0, 6.0, ((0, 4), (1, 4))),
    }


def reference(left_factors, right_factors, out_weight, out_bias, pair_grad):
    left_all = left_factors.reshape(L, CH, S).astype(jnp.float32)
    right_all = right_factors.reshape(L, CH, S).astype(jnp.float32)
    weight_f = out_weight.astype(jnp.float32)
    row_blocks = left_all.reshape(L // RES_DEV, RES_DEV, CH, S)
    grad_blocks = pair_grad.reshape(L // RES_DEV, RES_DEV, L, H)

    def advance(carried, inputs):
        weight_acc, right_acc = carried
        left_blk, grad_blk = inputs
        outer_mean = (jnp.einsum('ics,jes->ijce', left_blk, right_all) * (1.0 / S)).astype(jnp.bfloat16)
        outer_mean = lax.optimization_barrier(outer_mean)
        outer_f = outer_mean.astype(jnp.float32).reshape(RES_DEV, L, CH * CH)
        pair_blk = (jnp.einsum('ijk,kh->ijh', outer_f, weight_f) + out_bias).astype(jnp.bfloat16)
        grad_f = grad_blk.astype(jnp.float32)
        weight_acc = weight_acc + jnp.einsum('ijk,ijh->kh', outer_f, grad_f)
        outer_grad = jnp.einsum('ijh,kh->ijk', grad_f, weight_f).astype(jnp.bfloat16)
        outer_grad = lax.optimization_barrier(outer_grad)
        outer_grad = outer_grad.astype(jnp.float32).reshape(RES_DEV, L, CH, CH)
        left_part = jnp.einsum('ijce,jes->ics', outer_grad, right_all) * (1.0 / S)
        right_acc = right_acc + jnp.einsum('ijce,ics->jes', outer_grad, left_blk) * (1.0 / S)
        return (weight_acc, right_acc), (pair_blk, left_part)

    start = (jnp.zeros((CH * CH, H), jnp.float32), jnp.zeros((L, CH, S), jnp.float32))
    (weight_acc, right_acc), (pair_blocks, left_parts) = lax.scan(advance, start, (row_blocks, grad_blocks))
    pair_update = pair_blocks.reshape(L, L, H)
    grad_left = left_parts.reshape(N_ROW, RES_DEV, CH, S)
    grad_right = right_acc.reshape(N_COL, RES_DEV, CH, S)
    grad_weight = weight_acc / jnp.float32(L)
    return (pair_update, grad_left, grad_right, grad_weight)
```

```python
import jax
import jax.numpy as jnp
from jax import lax
from jax.experimental import pallas as pl
from jax.experimental.pallas import tpu as pltpu
from jax.sharding import PartitionSpec as P

BF = jnp.bfloat16
F32 = jnp.float32
VMEM = pl.BlockSpec(memory_space=pltpu.VMEM)
LANES = 128


def dot_nt(x, y):
    return lax.dot_general(x, y, (((1,), (1,)), ((), ())), preferred_element_type=F32)


def dot_tn(x, y):
    return lax.dot_general(x, y, (((0,), (0,)), ((), ())), preferred_element_type=F32)


def dot_nn(x, y):
    return lax.dot_general(x, y, (((1,), (0,)), ((), ())), preferred_element_type=F32)


def swap01(x):
    return jnp.swapaxes(x.astype(F32), 0, 1).astype(x.dtype)


def xor_groups(x, a, chan):
    n = x.shape[0] // (4 * chan)
    x4 = x.reshape(n, 4, chan, x.shape[-1])
    return jnp.concatenate([x4[:, p ^ a][:, None] for p in range(4)], axis=1).reshape(x.shape)


def lane_masks(rows, chan):
    group = lax.broadcasted_iota(jnp.int32, (rows, LANES), 1) // chan
    return (group % 2) == 1, (group // 2) == 1


def trade(xs, masks):
    low, high = masks
    u = [jnp.where(low, xs[a ^ 1], xs[a]) for a in range(4)]
    return [jnp.where(high, u[b ^ 2], u[b]) for b in range(4)]


def assemble(scratch, parts, axis, axis_size):
    me = lax.axis_index(axis)
    piece = parts[0].shape[0]
    for k in range(axis_size):
        scratch[pl.ds((me ^ k) * piece, piece)] = parts[k][...]


def hand_out(total, pieces, axis, axis_size):
    me = lax.axis_index(axis)
    piece = pieces[0].shape[0]
    for k in range(axis_size):
        pieces[k][...] = total[pl.ds((me ^ k) * piece, piece)].astype(pieces[k].dtype)


def call(kernel, outs, scratch, name, *operands):
    single = not isinstance(outs, (list, tuple))
    return pl.pallas_call(
        kernel,
        out_shape=outs,
        in_specs=[VMEM] * len(operands),
        out_specs=VMEM if single else [VMEM] * len(outs),
        scratch_shapes=list(scratch),
        compiler_params=pltpu.CompilerParams(vmem_limit_bytes=40 * 1024 * 1024),
        name=name,
    )(*operands)


def send_xor(pieces, axis, axis_size):
    return [pieces[0]] + [
        lax.ppermute(pieces[k], axis, [(d, d ^ k) for d in range(axis_size)])
        for k in range(1, axis_size)
    ]


def on_device(left_factors, right_factors, out_weight, out_bias, pair_grad):
    n_row = lax.axis_size("row")
    n_col = lax.axis_size("col")
    left, right = left_factors[0], right_factors[0]
    left_piece, chan, samples = left.shape
    right_piece = right.shape[0]
    rows, cols, width = pair_grad.shape
    pairs = chan * chan
    row4, chan4 = rows // 4, chan // 4
    inv_samples = 1.0 / samples
    struct = jax.ShapeDtypeStruct
    weight3 = out_weight.reshape(chan, chan, width)
    grad4 = pair_grad.reshape(row4, 4, cols, width)

    right_parts = send_xor([right] * n_row, "row", n_row)
    left_parts = send_xor([left] * n_col, "col", n_col)

    wide = 2 * LANES

    def outer_grad_kernel(grad_ref, weight_ref, z_ref, tmp):
        w = swap01(weight_ref[...]).reshape(pairs, width)
        masks = lane_masks(cols, chan)
        for blk in range(pairs // wide):
            for b in range(4):
                tmp[blk, b] = dot_nt(
                    grad_ref[:, b].reshape(row4 * cols, width),
                    xor_groups(w, b, chan)[blk * wide : (blk + 1) * wide],
                ).astype(BF)
            for n in range(row4):
                for h in range(2):
                    ys = trade(
                        [
                            tmp[blk, b, n * cols : (n + 1) * cols, h * LANES : (h + 1) * LANES]
                            for b in range(4)
                        ],
                        masks,
                    )
                    for a in range(4):
                        z_ref[2 * blk + h, a, :, n * LANES : (n + 1) * LANES] = ys[a]

    z = call(
        outer_grad_kernel,
        struct((chan4, 4, cols, rows * chan), BF),
        [pltpu.VMEM((pairs // wide, 4, row4 * cols, wide), BF)],
        "outer_grad",
        grad4,
        weight3,
    )

    def left_kernel(z_ref, *refs):
        b_refs, pieces, whole, total = refs[:n_row], refs[n_row : n_row + n_col], refs[-2], refs[-1]
        assemble(whole, b_refs, "row", n_row)
        be = swap01(whole[...]).reshape(chan4, 4, cols, samples)
        acc = None
        for a in range(4):
            d = dot_tn(
                z_ref[:, a].reshape(chan4 * cols, rows * chan),
                be[:, a].reshape(chan4 * cols, samples),
            )
            d = xor_groups(d, a, chan)
            acc = d if acc is None else acc + d
        total[...] = (acc * inv_samples).reshape(rows, chan, samples)
        hand_out(total, pieces, "col", n_col)

    left_pieces = call(
        left_kernel,
        [struct((left_piece, chan, samples), BF)] * n_col,
        [pltpu.VMEM((cols, chan, samples), BF), pltpu.VMEM((rows, chan, samples), F32)],
        "left_grad",
        z,
        *right_parts,
    )
    left_got = send_xor(left_pieces, "col", n_col)

    weight_piece = pairs // n_row

    def outer_mean_kernel(grad_ref, *refs):
        a_refs, b_refs = refs[:n_col], refs[n_col : n_col + n_row]
        y_ref = refs[n_col + n_row]
        pieces = refs[n_col + n_row + 1 : n_col + 2 * n_row + 1]
        a_whole, b_whole, tmp, total = refs[-4:]
        assemble(a_whole, a_refs, "col", n_col)
        assemble(b_whole, b_refs, "row", n_row)
        be = swap01(b_whole[...]).reshape(chan4, 4, cols, samples)
        am = a_whole[...].reshape(rows * chan, samples)
        masks = lane_masks(cols, chan)
        for blk in range(rows * chan // wide):
            for a in range(4):
                tmp[blk, a] = dot_nt(
                    be[:, a].reshape(chan4 * cols, samples),
                    xor_groups(am, a, chan)[blk * wide : (blk + 1) * wide],
                ).astype(BF)
            for e in range(chan4):
                for h in range(2):
                    ys = trade(
                        [
                            tmp[blk, a, e * cols : (e + 1) * cols, h * LANES : (h + 1) * LANES]
                            for a in range(4)
                        ],
                        masks,
                    )
                    for b in range(4):
                        y_ref[2 * blk + h, b, :, e * LANES : (e + 1) * LANES] = ys[b]
        acc = None
        for b in range(4):
            d = dot_tn(
                y_ref[:, b].reshape(row4 * cols, pairs),
                grad_ref[:, b].reshape(row4 * cols, width),
            )
            d = xor_groups(d, b, chan)
            acc = d if acc is None else acc + d
        acc = (acc * (inv_samples / (rows * n_row))).reshape(chan, chan, width)
        total[...] = jnp.swapaxes(acc, 0, 1).reshape(pairs, width)
        hand_out(total, pieces, "row", n_row)

    y, *weight_pieces = call(
        outer_mean_kernel,
        [struct((row4, 4, cols, pairs), BF)] + [struct((weight_piece, width), BF)] * n_row,
        [
            pltpu.VMEM((rows, chan, samples), BF),
            pltpu.VMEM((cols, chan, samples), BF),
            pltpu.VMEM((rows * chan // wide, 4, chan4 * cols, wide), BF),
            pltpu.VMEM((pairs, width), F32),
        ],
        "outer_mean",
        grad4,
        *left_parts,
        *right_parts,
    )
    weight_got = send_xor(weight_pieces, "row", n_row)

    def right_kernel(z_ref, *refs):
        a_refs, pieces, whole, total = refs[:n_col], refs[n_col : n_col + n_row], refs[-2], refs[-1]
        assemble(whole, a_refs, "col", n_col)
        am = whole[...].reshape(rows * chan, samples)
        for a in range(4):
            d = dot_nn(z_ref[:, a].reshape(chan4 * cols, rows * chan), xor_groups(am, a, chan))
            total[:, a] = d.reshape(chan4, cols, samples)
        d = jnp.swapaxes(total[...].reshape(chan, cols, samples), 0, 1) * inv_samples
        me = lax.axis_index("row")
        wholes = d.astype(BF)
        whole2 = refs[-3]
        whole2[...] = wholes
        for k in range(n_row):
            pieces[k][...] = whole2[pl.ds((me ^ k) * right_piece, right_piece)]

    right_pieces = call(
        right_kernel,
        [struct((right_piece, chan, samples), BF)] * n_row,
        [
            pltpu.VMEM((cols, chan, samples), BF),
            pltpu.VMEM((rows, chan, samples), BF),
            pltpu.VMEM((chan4, 4, cols, samples), F32),
        ],
        "right_grad",
        z,
        *left_parts,
    )
    right_got = send_xor(right_pieces, "row", n_row)

    def pair_kernel(y_ref, weight_ref, bias_ref, p_ref):
        w = swap01(weight_ref[...]).reshape(pairs, width)
        for b in range(4):
            d = dot_nn(y_ref[:, b].reshape(row4 * cols, pairs), xor_groups(w, b, chan))
            p_ref[:, b] = (d * inv_samples + bias_ref[...]).reshape(row4, cols, width).astype(BF)

    pair_update = call(
        pair_kernel,
        struct((row4, 4, cols, width), BF),
        [],
        "pair_update",
        y,
        weight3,
        out_bias.reshape(1, width),
    ).reshape(rows, cols, width)

    def add_up(parts):
        total = parts[0].astype(F32)
        for part in parts[1:]:
            total = total + part.astype(F32)
        return total

    weight_row = add_up(weight_got)
    col_me = lax.axis_index("col")
    row_me = lax.axis_index("row")
    fine = weight_piece // n_col
    weight_fine = [
        lax.dynamic_slice_in_dim(weight_row, (col_me ^ k) * fine, fine, 0) for k in range(n_col)
    ]
    weight_sum = add_up(send_xor(weight_fine, "col", n_col))
    col_parts = send_xor([weight_sum] * n_col, "col", n_col)
    mine = jnp.zeros((n_col, fine, width), F32)
    for k in range(n_col):
        mine = lax.dynamic_update_slice_in_dim(mine, col_parts[k][None], col_me ^ k, 0)
    mine = mine.reshape(weight_piece, width).astype(BF)
    row_parts = send_xor([mine] * n_row, "row", n_row)
    grad_weight = jnp.zeros((n_row, weight_piece, width), F32)
    for k in range(n_row):
        grad_weight = lax.dynamic_update_slice_in_dim(
            grad_weight, row_parts[k][None].astype(F32), row_me ^ k, 0
        )
    grad_weight = grad_weight.reshape(pairs, width)
    grad_left = add_up(left_got)[None]
    grad_right = add_up(right_got)[None]
    return (pair_update, grad_left, grad_right, grad_weight)


def solution(mesh):
    return jax.shard_map(
        on_device,
        mesh=mesh,
        in_specs=(
            P(("grp", "row"), "col", None, None),
            P(("grp", "col"), "row", None, None),
            P(),
            P(),
            P(("grp", "row"), "col", None),
        ),
        out_specs=(
            P(("grp", "row"), "col", None),
            P(("grp", "row"), "col", None, None),
            P(("grp", "col"), "row", None, None),
            P("grp", None),
        ),
        check_vma=False,
    )
```

```python
import jax
import jax.numpy as jnp
from jax import lax
from jax.experimental import pallas as pl
from jax.experimental.pallas import tpu as pltpu
from jax.sharding import PartitionSpec as P

BF = jnp.bfloat16
F32 = jnp.float32
VMEM = pl.BlockSpec(memory_space=pltpu.VMEM)
LANES = 128


def dot_nt(x, y):
    return lax.dot_general(x, y, (((1,), (1,)), ((), ())), preferred_element_type=F32)


def dot_tn(x, y):
    return lax.dot_general(x, y, (((0,), (0,)), ((), ())), preferred_element_type=F32)


def dot_nn(x, y):
    return lax.dot_general(x, y, (((1,), (0,)), ((), ())), preferred_element_type=F32)


def swap01(x):
    return jnp.swapaxes(x.astype(F32), 0, 1).astype(x.dtype)


def xor_groups(x, a, chan):
    n = x.shape[0] // (4 * chan)
    x4 = x.reshape(n, 4, chan, x.shape[-1])
    return jnp.concatenate([x4[:, p ^ a][:, None] for p in range(4)], axis=1).reshape(x.shape)


def lane_masks(rows, chan):
    group = lax.broadcasted_iota(jnp.int32, (rows, LANES), 1) // chan
    return (group % 2) == 1, (group // 2) == 1


def trade(xs, masks):
    low, high = masks
    u = [jnp.where(low, xs[a ^ 1], xs[a]) for a in range(4)]
    return [jnp.where(high, u[b ^ 2], u[b]) for b in range(4)]


def assemble(scratch, parts, axis, axis_size):
    me = lax.axis_index(axis)
    piece = parts[0].shape[0]
    for k in range(axis_size):
        scratch[pl.ds((me ^ k) * piece, piece)] = parts[k][...]


def hand_out(total, pieces, axis, axis_size):
    me = lax.axis_index(axis)
    piece = pieces[0].shape[0]
    for k in range(axis_size):
        pieces[k][...] = total[pl.ds((me ^ k) * piece, piece)].astype(pieces[k].dtype)


def hand_out_halves(total, keep, send, axis, axis_size):
    me = lax.axis_index(axis)
    piece = keep.shape[1]
    for k in range(axis_size):
        out = send if k % 2 else keep
        out[k // 2] = total[pl.ds((me ^ k) * piece, piece)].astype(out.dtype)


def call(kernel, outs, scratch, name, flops, *operands):
    single = not isinstance(outs, (list, tuple))
    return pl.pallas_call(
        kernel,
        out_shape=outs,
        in_specs=[VMEM] * len(operands),
        out_specs=VMEM if single else [VMEM] * len(outs),
        scratch_shapes=list(scratch),
        compiler_params=pltpu.CompilerParams(vmem_limit_bytes=24 * 1024 * 1024),
        cost_estimate=pl.CostEstimate(flops=flops, bytes_accessed=2**20, transcendentals=0),
        name=name,
    )(*operands)


def swap(x, axis, k):
    n = lax.axis_size(axis)
    return lax.ppermute(x, axis, [(d, d ^ k) for d in range(n)])


def after(x, *earlier):
    return lax.optimization_barrier((x, earlier))[0]


def bits_of(n):
    return [1 << s for s in range(n.bit_length() - 1)]


def gather_halves(own, axis, n):
    parts = {0: own}
    for bit in reversed(bits_of(n)):
        for k in sorted(parts):
            parts[k ^ bit] = swap(parts[k], axis, bit)
    return [parts[k] for k in range(n)]


def gather_direct(own, axis, n):
    return [own] + [swap(own, axis, k) for k in range(1, n)]


def tree_sum(parts):
    parts = [part.astype(F32) for part in parts]
    while len(parts) > 1:
        parts = [parts[i] + parts[i + 1] for i in range(0, len(parts), 2)]
    return parts[0]


def on_device(left_factors, right_factors, out_weight, out_bias, pair_grad):
    n_row = lax.axis_size("row")
    n_col = lax.axis_size("col")
    left, right = left_factors[0], right_factors[0]
    left_piece, chan, samples = left.shape
    right_piece = right.shape[0]
    rows, cols, width = pair_grad.shape
    pairs = chan * chan
    row4, chan4 = rows // 4, chan // 4
    inv_samples = 1.0 / samples
    flops = 2 * rows * cols * pairs * width
    wide = 2 * LANES
    half = n_row // 2
    weight_piece = pairs // n_row
    struct = jax.ShapeDtypeStruct
    weight3 = out_weight.reshape(chan, chan, width)
    grad4 = pair_grad.reshape(row4, 4, cols, width)

    right_parts = gather_halves(right, "row", n_row)
    left_parts = gather_direct(left, "col", n_col)

    def outer_grad_kernel(grad_ref, weight_ref, z_ref, tmp):
        w = swap01(weight_ref[...]).reshape(pairs, width)
        masks = lane_masks(cols, chan)
        for blk in range(pairs // wide):
            for b in range(4):
                tmp[blk, b] = dot_nt(
                    grad_ref[:, b].reshape(row4 * cols, width),
                    xor_groups(w, b, chan)[blk * wide : (blk + 1) * wide],
                ).astype(BF)
            for n in range(row4):
                for h in range(2):
                    ys = trade(
                        [
                            tmp[blk, b, n * cols : (n + 1) * cols, h * LANES : (h + 1) * LANES]
                            for b in range(4)
                        ],
                        masks,
                    )
                    for a in range(4):
                        z_ref[2 * blk + h, a, :, n * LANES : (n + 1) * LANES] = ys[a]

    z = call(
        outer_grad_kernel,
        struct((chan4, 4, cols, rows * chan), BF),
        [pltpu.VMEM((pairs // wide, 4, row4 * cols, wide), BF)],
        "outer_grad",
        flops,
        grad4,
        weight3,
    )

    def left_kernel(z_ref, *refs):
        b_refs, pieces, whole, total = refs[:n_row], refs[n_row : n_row + n_col], refs[-2], refs[-1]
        assemble(whole, b_refs, "row", n_row)
        be = swap01(whole[...]).reshape(chan4, 4, cols, samples)
        acc = None
        for a in range(4):
            d = dot_tn(
                z_ref[:, a].reshape(chan4 * cols, rows * chan),
                be[:, a].reshape(chan4 * cols, samples),
            )
            d = xor_groups(d, a, chan)
            acc = d if acc is None else acc + d
        total[...] = (acc * inv_samples).reshape(rows, chan, samples)
        hand_out(total, pieces, "col", n_col)

    left_pieces = call(
        left_kernel,
        [struct((left_piece, chan, samples), BF)] * n_col,
        [pltpu.VMEM((cols, chan, samples), BF), pltpu.VMEM((rows, chan, samples), F32)],
        "left_grad",
        flops,
        z,
        *right_parts,
    )
    left_parts[-1] = after(left_parts[-1], *left_pieces)

    def outer_mean_kernel(grad_ref, *refs):
        a_refs, b_refs = refs[:n_col], refs[n_col : n_col + n_row]
        y_ref, keep, send = refs[n_col + n_row : n_col + n_row + 3]
        a_whole, b_whole, tmp, total = refs[-4:]
        assemble(a_whole, a_refs, "col", n_col)
        assemble(b_whole, b_refs, "row", n_row)
        be = swap01(b_whole[...]).reshape(chan4, 4, cols, samples)
        am = a_whole[...].reshape(rows * chan, samples)
        masks = lane_masks(cols, chan)
        for blk in range(rows * chan // wide):
            for a in range(4):
                tmp[blk, a] = dot_nt(
                    be[:, a].reshape(chan4 * cols, samples),
                    xor_groups(am, a, chan)[blk * wide : (blk + 1) * wide],
                ).astype(BF)
            for e in range(chan4):
                for h in range(2):
                    ys = trade(
                        [
                            tmp[blk, a, e * cols : (e + 1) * cols, h * LANES : (h + 1) * LANES]
                            for a in range(4)
                        ],
                        masks,
                    )
                    for b in range(4):
                        y_ref[2 * blk + h, b, :, e * LANES : (e + 1) * LANES] = ys[b]
        acc = None
        for b in range(4):
            d = dot_tn(
                y_ref[:, b].reshape(row4 * cols, pairs),
                grad_ref[:, b].reshape(row4 * cols, width),
            )
            d = xor_groups(d, b, chan)
            acc = d if acc is None else acc + d
        acc = (acc * (inv_samples / (rows * n_row))).reshape(chan, chan, width)
        total[...] = jnp.swapaxes(acc, 0, 1).reshape(pairs, width)
        hand_out_halves(total, keep, send, "row", n_row)

    y, weight_keep, weight_send = call(
        outer_mean_kernel,
        [
            struct((row4, 4, cols, pairs), BF),
            struct((half, weight_piece, width), F32),
            struct((half, weight_piece, width), BF),
        ],
        [
            pltpu.VMEM((rows, chan, samples), BF),
            pltpu.VMEM((cols, chan, samples), BF),
            pltpu.VMEM((rows * chan // wide, 4, chan4 * cols, wide), BF),
            pltpu.VMEM((pairs, width), F32),
        ],
        "outer_mean",
        2 * flops,
        grad4,
        *left_parts,
        *right_parts,
    )

    def right_kernel(z_ref, *refs):
        a_refs, (keep, send) = refs[:n_col], refs[n_col : n_col + 2]
        whole, total, turned = refs[-3:]
        assemble(whole, a_refs, "col", n_col)
        am = whole[...].reshape(rows * chan, samples)
        for a in range(4):
            d = dot_nn(z_ref[:, a].reshape(chan4 * cols, rows * chan), xor_groups(am, a, chan))
            total[:, a] = d.reshape(chan4, cols, samples)
        turned[...] = jnp.swapaxes(total[...].reshape(chan, cols, samples), 0, 1) * inv_samples
        hand_out_halves(turned, keep, send, "row", n_row)

    right_keep, right_send = call(
        right_kernel,
        [
            struct((half, right_piece, chan, samples), F32),
            struct((half, right_piece, chan, samples), BF),
        ],
        [
            pltpu.VMEM((rows, chan, samples), BF),
            pltpu.VMEM((chan4, 4, cols, samples), F32),
            pltpu.VMEM((cols, chan, samples), F32),
        ],
        "right_grad",
        flops,
        after(z, weight_send),
        *left_parts,
    )

    def halve_kernel(w_keep, w_got, r_keep, r_got, w_next, w_send, r_next, r_send):
        n = w_keep.shape[0]
        for k in range(n):
            w_out, r_out = (w_send, r_send) if k % 2 else (w_next, r_next)
            w_out[k // 2] = (w_keep[k] + w_got[k].astype(F32)).astype(w_out.dtype)
            r_out[k // 2] = (r_keep[k] + r_got[k].astype(F32)).astype(r_out.dtype)

    for bit in bits_of(n_row)[:-1]:
        weight_got = swap(weight_send, "row", bit)
        right_got = swap(right_send, "row", bit)
        half = half // 2
        weight_keep, weight_send, right_keep, right_send = call(
            halve_kernel,
            [
                struct((half, weight_piece, width), F32),
                struct((half, weight_piece, width), BF),
                struct((half, right_piece, chan, samples), F32),
                struct((half, right_piece, chan, samples), BF),
            ],
            [],
            "halve_row_%d" % bit,
            2**20,
            weight_keep,
            weight_got,
            right_keep,
            right_got,
        )

    weight_got = swap(weight_send, "row", n_row // 2)
    right_got = swap(right_send, "row", n_row // 2)
    left_pieces = [after(piece, weight_send) for piece in left_pieces]
    left_got = [left_pieces[0]] + [swap(left_pieces[k], "col", k) for k in range(1, n_col)]

    def last_kernel(w_keep, w_got, r_keep, r_got, w_out, r_out):
        w_out[...] = (w_keep[0] + w_got[0].astype(F32)).astype(w_out.dtype)
        r_out[...] = r_keep[...] + r_got[...].astype(F32)

    weight_own, grad_right = call(
        last_kernel,
        [struct((weight_piece, width), BF), struct((1, right_piece, chan, samples), F32)],
        [],
        "halve_row_last",
        2**20,
        weight_keep,
        weight_got,
        right_keep,
        right_got,
    )
    weight_cols = gather_direct(weight_own, "col", n_col)

    def pair_kernel(y_ref, weight_ref, bias_ref, p_ref):
        w = swap01(weight_ref[...]).reshape(pairs, width)
        for b in range(4):
            d = dot_nn(y_ref[:, b].reshape(row4 * cols, pairs), xor_groups(w, b, chan))
            p_ref[:, b] = (d * inv_samples + bias_ref[...]).reshape(row4, cols, width).astype(BF)

    pair_update = call(
        pair_kernel,
        struct((row4, 4, cols, width), BF),
        [],
        "pair_update",
        flops,
        after(y, weight_own),
        weight3,
        out_bias.reshape(1, width),
    )
    grad_left = tree_sum(left_got)[None]
    weight_cols[-1] = after(weight_cols[-1], pair_update, grad_left)

    def col_sum_kernel(*refs):
        refs[-1][...] = tree_sum([ref[...] for ref in refs[:-1]]).astype(BF)

    weight_sum = call(
        col_sum_kernel, struct((weight_piece, width), BF), [], "weight_col_sum", 2**20, *weight_cols
    )
    weight_rows = gather_halves(weight_sum, "row", n_row)

    def place_kernel(*refs):
        me = lax.axis_index("row")
        for k in range(n_row):
            refs[-1][pl.ds((me ^ k) * weight_piece, weight_piece)] = refs[k][...].astype(F32)

    grad_weight = call(
        place_kernel, struct((pairs, width), F32), [], "weight_place", 2**20, *weight_rows
    )
    return (pair_update.reshape(rows, cols, width), grad_left, grad_right, grad_weight)


def solution(mesh):
    return jax.shard_map(
        on_device,
        mesh=mesh,
        in_specs=(
            P(("grp", "row"), "col", None, None),
            P(("grp", "col"), "row", None, None),
            P(),
            P(),
            P(("grp", "row"), "col", None),
        ),
        out_specs=(
            P(("grp", "row"), "col", None),
            P(("grp", "row"), "col", None, None),
            P(("grp", "col"), "row", None, None),
            P("grp", None),
        ),
        check_vma=False,
    )
```

```python
import jax
import jax.numpy as jnp
from jax import lax
from jax.experimental import pallas as pl
from jax.experimental.pallas import tpu as pltpu
from jax.sharding import PartitionSpec as P

BF = jnp.bfloat16
F32 = jnp.float32
VMEM = pl.BlockSpec(memory_space=pltpu.VMEM)
LANES = 128


def dot_nt(x, y):
    return lax.dot_general(x, y, (((1,), (1,)), ((), ())), preferred_element_type=F32)


def dot_tn(x, y):
    return lax.dot_general(x, y, (((0,), (0,)), ((), ())), preferred_element_type=F32)


def dot_nn(x, y):
    return lax.dot_general(x, y, (((1,), (0,)), ((), ())), preferred_element_type=F32)


def swap01(x):
    return jnp.swapaxes(x.astype(F32), 0, 1).astype(x.dtype)


def xor_groups(x, a, chan):
    n = x.shape[0] // (4 * chan)
    x4 = x.reshape(n, 4, chan, x.shape[-1])
    return jnp.concatenate([x4[:, p ^ a][:, None] for p in range(4)], axis=1).reshape(x.shape)


def lane_masks(rows, chan):
    group = lax.broadcasted_iota(jnp.int32, (rows, LANES), 1) // chan
    return (group % 2) == 1, (group // 2) == 1


def trade(xs, masks):
    low, high = masks
    u = [jnp.where(low, xs[a ^ 1], xs[a]) for a in range(4)]
    return [jnp.where(high, u[b ^ 2], u[b]) for b in range(4)]


def assemble(scratch, parts, first, me):
    piece = parts[0].shape[0]
    count = scratch.shape[0] // piece
    for k, part in enumerate(parts):
        scratch[pl.ds(((me ^ (first + k)) % count) * piece, piece)] = part[...]


def call(kernel, outs, scratch, name, *operands, cost=1, hbm_in=(), hbm_out=()):
    hbm = pl.BlockSpec(memory_space=pltpu.HBM)
    return pl.pallas_call(
        kernel,
        out_shape=outs,
        in_specs=[hbm if i in hbm_in else VMEM for i in range(len(operands))],
        out_specs=[hbm if i in hbm_out else VMEM for i in range(len(outs))],
        scratch_shapes=list(scratch),
        compiler_params=pltpu.CompilerParams(vmem_limit_bytes=24 * 1024 * 1024),
        cost_estimate=pl.CostEstimate(flops=cost * 2**30, bytes_accessed=2**16, transcendentals=0),
        name=name,
    )(*operands)


def hand_out_halves(total, keep, send, me):
    piece = keep.shape[1]
    for k in range(total.shape[0] // piece):
        out = send if k % 2 else keep
        out[k // 2] = total[pl.ds((me ^ k) * piece, piece)].astype(out.dtype)


def swap(x, axis, k):
    n = lax.axis_size(axis)
    return lax.ppermute(x, axis, [(d, d ^ k) for d in range(n)])


def swap_all(pieces, axis):
    return [pieces[0]] + [swap(pieces[k], axis, k) for k in range(1, len(pieces))]


def bits_of(n):
    return [1 << s for s in range(n.bit_length() - 1)]


def gather_halves(own, axis):
    n = lax.axis_size(axis)
    parts = {0: own}
    for bit in reversed(bits_of(n)):
        for k in sorted(parts):
            parts[k ^ bit] = swap(parts[k], axis, bit)
    return [parts[k] for k in range(n)]


def after(x, *earlier):
    return lax.optimization_barrier((x, earlier))[0]


def tree_sum(parts):
    parts = [part.astype(F32) for part in parts]
    while len(parts) > 1:
        parts = [parts[i] + parts[i + 1] for i in range(0, len(parts), 2)]
    return parts[0]


def on_device(left_factors, right_factors, out_weight, out_bias, pair_grad):
    n_row = lax.axis_size("row")
    n_col = lax.axis_size("col")
    left, right = left_factors[0], right_factors[0]
    left_piece, chan, samples = left.shape
    right_piece = right.shape[0]
    rows, cols, width = pair_grad.shape
    pairs = chan * chan
    row4, chan4 = rows // 4, chan // 4
    half4 = row4 // 2
    near, half = n_col // 2, n_row // 2
    inv_samples = 1.0 / samples
    wide = 2 * LANES
    weight_piece = pairs // n_row
    struct = jax.ShapeDtypeStruct
    weight3 = out_weight.reshape(chan, chan, width)
    grad4 = pair_grad.reshape(row4, 4, cols, width)

    left_parts = gather_halves(left, "col")
    right_parts = gather_halves(right, "row")

    def stage_kernel(grad_hbm, weight_hbm, left_hbm, right_hbm, grad, weight_e, left, right, *scr):
        weight, sems = scr
        copies = [
            pltpu.make_async_copy(source, target, sems.at[i])
            for i, (source, target) in enumerate(
                [(weight_hbm, weight), (left_hbm, left), (right_hbm, right), (grad_hbm, grad)]
            )
        ]
        for copy in copies:
            copy.start()
        copies[0].wait()
        weight_e[...] = swap01(weight[...]).reshape(pairs, width)
        for copy in copies[1:]:
            copy.wait()

    grad_vmem, weight_e, left_parts[0], right_parts[0] = call(
        stage_kernel,
        [
            struct(grad4.shape, BF),
            struct((pairs, width), BF),
            struct(left.shape, BF),
            struct(right.shape, BF),
        ],
        [pltpu.VMEM(weight3.shape, BF), pltpu.SemaphoreType.DMA((4,))],
        "stage",
        *[pltpu.with_memory_space_constraint(x, pltpu.HBM) for x in (grad4, weight3, left, right)],
        hbm_in=(0, 1, 2, 3),
    )

    def outer_mean(a_whole, be, grad_ref, y_ref, tmp, group, masks):
        am = a_whole[...].reshape(rows * chan // 2, samples)
        for blk in range(rows * chan // 2 // wide):
            for a in range(4):
                tmp[blk, a] = dot_nt(
                    be[:, a].reshape(chan4 * cols, samples),
                    xor_groups(am, a, chan)[blk * wide : (blk + 1) * wide],
                ).astype(BF)
            for e in range(chan4):
                for h in range(2):
                    ys = trade(
                        [
                            tmp[blk, a, e * cols : (e + 1) * cols, h * LANES : (h + 1) * LANES]
                            for a in range(4)
                        ],
                        masks,
                    )
                    for b in range(4):
                        y_ref[2 * blk + h, b, :, e * LANES : (e + 1) * LANES] = ys[b]
        acc = None
        for b in range(4):
            d = dot_tn(
                y_ref[:, b].reshape(half4 * cols, pairs),
                grad_ref[pl.ds(group * half4, half4), b].reshape(half4 * cols, width),
            )
            d = xor_groups(d, b, chan)
            acc = d if acc is None else acc + d
        return acc

    mean_scratch = [
        pltpu.VMEM((rows // 2, chan, samples), BF),
        pltpu.VMEM((rows * chan // 2 // wide, 4, chan4 * cols, wide), BF),
    ]

    def near_kernel(grad_ref, *refs):
        a_refs, b_refs = refs[:near], refs[near : near + n_row]
        y_ref, weight_ref, be_ref, a_whole, tmp, b_whole = refs[near + n_row :]
        me = lax.axis_index("col")
        assemble(a_whole, a_refs, 0, me)
        assemble(b_whole, b_refs, 0, lax.axis_index("row"))
        be = swap01(b_whole[...]).reshape(chan4, 4, cols, samples)
        be_ref[...] = be
        weight_ref[...] = outer_mean(
            a_whole, be, grad_ref, y_ref, tmp, me // near, lane_masks(cols, chan)
        )

    y_struct = struct((half4, 4, cols, pairs), BF)
    y_near, weight_near, right_e = call(
        near_kernel,
        [y_struct, struct((pairs, width), F32), struct((chan4, 4, cols, samples), BF)],
        mean_scratch + [pltpu.VMEM((cols, chan, samples), BF)],
        "outer_mean_near",
        grad_vmem,
        *left_parts[:near],
        *right_parts,
    )

    def far_kernel(grad_ref, be_ref, near_ref, *refs):
        a_refs, y_ref = refs[:near], refs[near]
        keep, send, a_whole, tmp, total = refs[near + 1 :]
        me = lax.axis_index("col")
        assemble(a_whole, a_refs, near, me)
        acc = outer_mean(
            a_whole, be_ref, grad_ref, y_ref, tmp, 1 - me // near, lane_masks(cols, chan)
        )
        acc = (acc + near_ref[...]) * (inv_samples / (rows * n_row))
        total[...] = jnp.swapaxes(acc.reshape(chan, chan, width), 0, 1).reshape(pairs, width)
        hand_out_halves(total, keep, send, lax.axis_index("row"))

    y_far, weight_keep, weight_send = call(
        far_kernel,
        [y_struct] + [struct((half, weight_piece, width), dtype) for dtype in (F32, BF)],
        mean_scratch + [pltpu.VMEM((pairs, width), F32)],
        "outer_mean_far",
        grad_vmem,
        right_e,
        weight_near,
        *left_parts[near:],
    )
    def outer_grad_kernel(grad_ref, weight_ref, z_ref, tmp):
        w = weight_ref[...]
        masks = lane_masks(cols, chan)
        for blk in range(pairs // wide):
            for b in range(4):
                tmp[blk, b] = dot_nt(
                    grad_ref[:, b].reshape(row4 * cols, width),
                    xor_groups(w, b, chan)[blk * wide : (blk + 1) * wide],
                ).astype(BF)
            for n in range(row4):
                for h in range(2):
                    ys = trade(
                        [
                            tmp[blk, b, n * cols : (n + 1) * cols, h * LANES : (h + 1) * LANES]
                            for b in range(4)
                        ],
                        masks,
                    )
                    for a in range(4):
                        z_ref[2 * blk + h, a, :, n * LANES : (n + 1) * LANES] = ys[a]

    (z,) = call(
        outer_grad_kernel,
        [struct((chan4, 4, cols, rows * chan), BF)],
        [pltpu.VMEM((pairs // wide, 4, row4 * cols, wide), BF)],
        "outer_grad",
        after(grad_vmem, weight_send),
        weight_e,
        cost=4,
    )

    def halve_kernel(keep, got, next_keep, next_send):
        for k in range(keep.shape[0]):
            out = next_send if k % 2 else next_keep
            out[k // 2] = (keep[k] + got[k].astype(F32)).astype(out.dtype)

    def halve(keep, got, name):
        shape = (keep.shape[0] // 2,) + keep.shape[1:]
        return call(
            halve_kernel, [struct(shape, dtype) for dtype in (F32, BF)], [], name, keep, got
        )

    for bit in bits_of(n_row)[:-1]:
        weight_got = after(swap(weight_send, "row", bit), z)
        weight_keep, weight_send = halve(weight_keep, weight_got, "weight_halve_%d" % bit)

    def left_kernel(z_ref, be_ref, keep, send, total):
        acc = None
        for a in range(4):
            d = dot_tn(
                z_ref[:, a].reshape(chan4 * cols, rows * chan),
                be_ref[:, a].reshape(chan4 * cols, samples),
            )
            d = xor_groups(d, a, chan)
            acc = d if acc is None else acc + d
        total[...] = (acc * inv_samples).reshape(rows, chan, samples)
        hand_out_halves(total, keep, send, lax.axis_index("col"))

    left_keep, left_send = call(
        left_kernel,
        [struct((near, left_piece, chan, samples), dtype) for dtype in (F32, BF)],
        [pltpu.VMEM((rows, chan, samples), F32)],
        "left_grad",
        after(z, weight_send),
        right_e,
        cost=3,
    )

    def right_kernel(z_ref, *refs):
        a_refs, (keep, send, whole, total, turned) = refs[:n_col], refs[n_col:]
        assemble(whole, a_refs, 0, lax.axis_index("col"))
        am = whole[...].reshape(rows * chan, samples)
        for a in range(4):
            d = dot_nn(z_ref[:, a].reshape(chan4 * cols, rows * chan), xor_groups(am, a, chan))
            total[:, a] = d.reshape(chan4, cols, samples)
        turned[...] = jnp.swapaxes(total[...].reshape(chan, cols, samples), 0, 1) * inv_samples
        hand_out_halves(turned, keep, send, lax.axis_index("row"))

    right_keep, right_send = call(
        right_kernel,
        [struct((half, right_piece, chan, samples), dtype) for dtype in (F32, BF)],
        [
            pltpu.VMEM((rows, chan, samples), BF),
            pltpu.VMEM((chan4, 4, cols, samples), F32),
            pltpu.VMEM((cols, chan, samples), F32),
        ],
        "right_grad",
        after(z, left_send),
        *left_parts,
        cost=3,
    )

    def last_kernel(keep, got, out):
        out[...] = (keep[0] + got[0].astype(F32)).astype(BF)

    (weight_own,) = call(
        last_kernel,
        [struct((weight_piece, width), BF)],
        [],
        "weight_row_sum",
        weight_keep,
        after(swap(weight_send, "row", half), right_send),
    )
    col_got = swap_all([weight_own] * n_col, "col")

    for bit in bits_of(n_col)[:-1]:
        left_got = after(swap(left_send, "col", bit), weight_own)
        left_keep, left_send = halve(left_keep, left_got, "left_halve_%d" % bit)
    left_got = swap(left_send, "col", near)

    for bit in bits_of(n_row)[:-1]:
        right_got = after(swap(right_send, "row", bit), left_send)
        right_keep, right_send = halve(right_keep, right_got, "right_halve_%d" % bit)
    right_got = swap(right_send, "row", half)


    def pair_kernel(near_ref, far_ref, weight_ref, bias_ref, p_hbm, p_ref, sem):
        me = lax.axis_index("col")
        copies = []
        for part, y_ref in enumerate((near_ref, far_ref)):
            group = part ^ (me // near)
            for b in range(4):
                d = dot_nn(
                    y_ref[:, b].reshape(half4 * cols, pairs), xor_groups(weight_ref[...], b, chan)
                )
                d = d * inv_samples + bias_ref[...]
                p_ref[part, :, b] = d.reshape(half4, cols, width).astype(BF)
            copies.append(
                pltpu.make_async_copy(
                    p_ref.at[part], p_hbm.at[pl.ds(group * half4, half4)], sem.at[part]
                )
            )
            copies[-1].start()
        for copy in copies:
            copy.wait()

    (pair_update,) = call(
        pair_kernel,
        [struct((row4, 4, cols, width), BF)],
        [pltpu.VMEM((2, half4, 4, cols, width), BF), pltpu.SemaphoreType.DMA((2,))],
        "pair_update",
        after(y_near, right_send, left_send),
        y_far,
        weight_e,
        out_bias.reshape(1, width),
        cost=16,
        hbm_out=(0,),
    )


    def col_sum_kernel(*refs):
        refs[-1][...] = tree_sum([ref[...] for ref in refs[:-1]]).astype(BF)

    (weight_sum,) = call(
        col_sum_kernel, [struct((weight_piece, width), BF)], [], "weight_col_sum", *col_got[:-1], after(col_got[-1], pair_update)
    )
    weight_rows = swap_all([weight_sum] * n_row, "row")

    def totals_kernel(l_keep, l_got, r_keep, r_got, l_out, r_out):
        l_out[...] = l_keep[...] + l_got[...].astype(F32)
        r_out[...] = r_keep[...] + r_got[...].astype(F32)

    grad_left, grad_right = call(
        totals_kernel,
        [
            struct((1, left_piece, chan, samples), F32),
            struct((1, right_piece, chan, samples), F32),
        ],
        [],
        "left_right_totals",
        after(left_keep, weight_sum),
        left_got,
        right_keep,
        right_got,
    )

    def place_kernel(*refs):
        me = lax.axis_index("row")
        for k in range(n_row):
            refs[-1][pl.ds((me ^ k) * weight_piece, weight_piece)] = refs[k][...].astype(F32)

    weight_rows[-1] = after(weight_rows[-1], grad_right)
    (grad_weight,) = call(
        place_kernel, [struct((pairs, width), F32)], [], "weight_place", *weight_rows
    )
    return (pair_update.reshape(rows, cols, width), grad_left, grad_right, grad_weight)


def solution(mesh):
    return jax.shard_map(
        on_device,
        mesh=mesh,
        in_specs=(
            P(("grp", "row"), "col", None, None),
            P(("grp", "col"), "row", None, None),
            P(),
            P(),
            P(("grp", "row"), "col", None),
        ),
        out_specs=(
            P(("grp", "row"), "col", None),
            P(("grp", "row"), "col", None, None),
            P(("grp", "col"), "row", None, None),
            P("grp", None),
        ),
        check_vma=False,
    )
```

```python
import jax
import jax.numpy as jnp
from jax import lax
from jax.experimental import pallas as pl
from jax.experimental.pallas import tpu as pltpu
from jax.sharding import PartitionSpec as P

BF = jnp.bfloat16
F32 = jnp.float32
VMEM = pl.BlockSpec(memory_space=pltpu.VMEM)
LANES = 128


def dot_nt(x, y):
    return lax.dot_general(x, y, (((1,), (1,)), ((), ())), preferred_element_type=F32)


def dot_tn(x, y):
    return lax.dot_general(x, y, (((0,), (0,)), ((), ())), preferred_element_type=F32)


def dot_nn(x, y):
    return lax.dot_general(x, y, (((1,), (0,)), ((), ())), preferred_element_type=F32)


def swap01(x):
    return jnp.swapaxes(x.astype(F32), 0, 1).astype(x.dtype)


def xor_groups(x, a, chan):
    n = x.shape[0] // (4 * chan)
    x4 = x.reshape(n, 4, chan, x.shape[-1])
    return jnp.concatenate([x4[:, p ^ a][:, None] for p in range(4)], axis=1).reshape(x.shape)


def lane_masks(rows, chan):
    group = lax.broadcasted_iota(jnp.int32, (rows, LANES), 1) // chan
    return (group % 2) == 1, (group // 2) == 1


def trade(xs, masks):
    low, high = masks
    u = [jnp.where(low, xs[a ^ 1], xs[a]) for a in range(4)]
    return [jnp.where(high, u[b ^ 2], u[b]) for b in range(4)]


def assemble(scratch, parts, first, me):
    piece = parts[0].shape[0]
    count = scratch.shape[0] // piece
    for k, part in enumerate(parts):
        scratch[pl.ds(((me ^ (first + k)) % count) * piece, piece)] = part[...]


def call(kernel, outs, scratch, name, *operands, cost=1, hbm_in=(), hbm_out=()):
    hbm = pl.BlockSpec(memory_space=pltpu.HBM)
    return pl.pallas_call(
        kernel,
        out_shape=outs,
        in_specs=[hbm if i in hbm_in else VMEM for i in range(len(operands))],
        out_specs=[hbm if i in hbm_out else VMEM for i in range(len(outs))],
        scratch_shapes=list(scratch),
        compiler_params=pltpu.CompilerParams(vmem_limit_bytes=24 * 1024 * 1024),
        cost_estimate=pl.CostEstimate(flops=cost * 2**30, bytes_accessed=2**16, transcendentals=0),
        name=name,
    )(*operands)


def hand_out_halves(total, keep, send, me):
    piece = keep.shape[1]
    for k in range(total.shape[0] // piece):
        out = send if k % 2 else keep
        out[k // 2] = total[pl.ds((me ^ k) * piece, piece)].astype(out.dtype)


def swap(x, axis, k):
    n = lax.axis_size(axis)
    return lax.ppermute(x, axis, [(d, d ^ k) for d in range(n)])


def swap_all(pieces, axis):
    return [pieces[0]] + [swap(pieces[k], axis, k) for k in range(1, len(pieces))]


def bits_of(n):
    return [1 << s for s in range(n.bit_length() - 1)]


def gather_halves(own, axis):
    n = lax.axis_size(axis)
    parts = {0: own}
    for bit in reversed(bits_of(n)):
        for k in sorted(parts):
            parts[k ^ bit] = swap(parts[k], axis, bit)
    return [parts[k] for k in range(n)]


def gather_far(own, axis):
    n = lax.axis_size(axis)
    return {0: own, n // 2: swap(own, axis, n // 2)}


def gather_rest(parts, axis):
    n = lax.axis_size(axis)
    for bit in reversed(bits_of(n)[:-1]):
        for k in sorted(parts):
            parts[k ^ bit] = swap(parts[k], axis, bit)
    return [parts[k] for k in range(n)]


def after(x, *earlier):
    return lax.optimization_barrier((x, earlier))[0]


def tree_sum(parts):
    parts = [part.astype(F32) for part in parts]
    while len(parts) > 1:
        parts = [parts[i] + parts[i + 1] for i in range(0, len(parts), 2)]
    return parts[0]


def on_device(left_factors, right_factors, out_weight, out_bias, pair_grad):
    n_row = lax.axis_size("row")
    n_col = lax.axis_size("col")
    left, right = left_factors[0], right_factors[0]
    left_piece, chan, samples = left.shape
    right_piece = right.shape[0]
    rows, cols, width = pair_grad.shape
    pairs = chan * chan
    row4, chan4 = rows // 4, chan // 4
    half4 = row4 // 2
    near, half = n_col // 2, n_row // 2
    inv_samples = 1.0 / samples
    wide = 2 * LANES
    weight_piece = pairs // n_row
    struct = jax.ShapeDtypeStruct
    weight3 = out_weight.reshape(chan, chan, width)
    grad4 = pair_grad.reshape(row4, 4, cols, width)

    left_parts = gather_far(left, "col")
    right_parts = gather_halves(right, "row")

    def tile(q, m, h):
        return q[m * cols : (m + 1) * cols, h * LANES : (h + 1) * LANES]

    def stage_kernel(grad_hbm, weight_hbm, left_hbm, right_hbm, grad, weight_e, left, right, *scr):
        weight, sems = scr
        copies = [
            pltpu.make_async_copy(source, target, sems.at[i])
            for i, (source, target) in enumerate(
                [(weight_hbm, weight), (left_hbm, left), (right_hbm, right), (grad_hbm, grad)]
            )
        ]
        for copy in copies:
            copy.start()
        copies[0].wait()
        weight_e[...] = swap01(weight[...]).reshape(pairs, width)
        for copy in copies[1:]:
            copy.wait()

    grad_vmem, weight_e, left_vmem, right_parts[0] = call(
        stage_kernel,
        [
            struct(grad4.shape, BF),
            struct((pairs, width), BF),
            struct(left.shape, BF),
            struct(right.shape, BF),
        ],
        [pltpu.VMEM(weight3.shape, BF), pltpu.SemaphoreType.DMA((4,))],
        "stage",
        *[pltpu.with_memory_space_constraint(x, pltpu.HBM) for x in (grad4, weight3, left, right)],
        hbm_in=(0, 1, 2, 3),
    )

    def outer_grad_kernel(grad_ref, weight_ref, z_ref):
        masks = lane_masks(cols, chan)
        ws = [xor_groups(weight_ref[...], b, chan) for b in range(4)]
        for blk in range(pairs // wide):
            for n in range(0, row4, 4):
                qs = [
                    dot_nt(
                        grad_ref[n : n + 4, b].reshape(4 * cols, width),
                        ws[b][blk * wide : (blk + 1) * wide],
                    ).astype(BF)
                    for b in range(4)
                ]
                for m, h in [(m, h) for m in range(4) for h in range(2)]:
                    ys = trade([tile(q, m, h) for q in qs], masks)
                    for a in range(4):
                        z_ref[2 * blk + h, a, :, (n + m) * LANES : (n + m + 1) * LANES] = ys[a]

    (z,) = call(
        outer_grad_kernel,
        [struct((chan4, 4, cols, rows * chan), BF)],
        [],
        "outer_grad",
        after(grad_vmem, right_parts[n_row // 2]),
        weight_e,
        cost=0,
    )

    left_parts[near] = after(left_parts[near], z)
    left_parts = gather_rest(left_parts, "col")
    left_parts[0] = left_vmem

    def outer_mean(a_whole, be, grad_ref, y_ref, group, masks):
        am = a_whole[...].reshape(rows * chan // 2, samples)
        ams = [xor_groups(am, a, chan) for a in range(4)]
        for blk in range(rows * chan // 2 // wide):
            for e in range(0, chan4, 4):
                qs = [
                    dot_nt(
                        be[e : e + 4, a].reshape(4 * cols, samples),
                        ams[a][blk * wide : (blk + 1) * wide],
                    ).astype(BF)
                    for a in range(4)
                ]
                for m, h in [(m, h) for m in range(4) for h in range(2)]:
                    ys = trade([tile(q, m, h) for q in qs], masks)
                    for b in range(4):
                        y_ref[2 * blk + h, b, :, (e + m) * LANES : (e + m + 1) * LANES] = ys[b]
        acc = None
        for b in range(4):
            g = grad_ref[pl.ds(group * half4, half4), b].reshape(half4 * cols, width)
            d = dot_nn(jnp.transpose(g), y_ref[:, b].reshape(half4 * cols, pairs))
            d = xor_groups(jnp.transpose(d), b, chan)
            acc = d if acc is None else acc + d
        return acc

    mean_scratch = [pltpu.VMEM((rows // 2, chan, samples), BF)]

    def near_kernel(grad_ref, *refs):
        a_refs, b_refs = refs[:near], refs[near : near + n_row]
        y_ref, weight_ref, be_ref, a_whole, b_whole = refs[near + n_row :]
        me = lax.axis_index("col")
        assemble(a_whole, a_refs, 0, me)
        assemble(b_whole, b_refs, 0, lax.axis_index("row"))
        be = swap01(b_whole[...]).reshape(chan4, 4, cols, samples)
        be_ref[...] = be
        weight_ref[...] = outer_mean(
            a_whole, be, grad_ref, y_ref, me // near, lane_masks(cols, chan)
        )

    y_struct = struct((half4, 4, cols, pairs), BF)
    y_near, weight_near, right_e = call(
        near_kernel,
        [y_struct, struct((pairs, width), F32), struct((chan4, 4, cols, samples), BF)],
        mean_scratch + [pltpu.VMEM((cols, chan, samples), BF)],
        "outer_mean_near",
        grad_vmem,
        *left_parts[:near],
        *right_parts,
    )

    def far_kernel(grad_ref, be_ref, near_ref, *refs):
        a_refs, y_ref = refs[:near], refs[near]
        keep, send, a_whole, total = refs[near + 1 :]
        me = lax.axis_index("col")
        assemble(a_whole, a_refs, near, me)
        acc = outer_mean(
            a_whole, be_ref, grad_ref, y_ref, 1 - me // near, lane_masks(cols, chan)
        )
        acc = (acc + near_ref[...]) * (inv_samples / (rows * n_row))
        total[...] = jnp.swapaxes(acc.reshape(chan, chan, width), 0, 1).reshape(pairs, width)
        hand_out_halves(total, keep, send, lax.axis_index("row"))

    y_far, weight_keep, weight_send = call(
        far_kernel,
        [y_struct] + [struct((half, weight_piece, width), F32)] * 2,
        mean_scratch + [pltpu.VMEM((pairs, width), F32)],
        "outer_mean_far",
        grad_vmem,
        right_e,
        weight_near,
        *left_parts[near:],
    )
    def halve_kernel(keep, got, next_keep, next_send):
        for k in range(keep.shape[0]):
            out = next_send if k % 2 else next_keep
            out[k // 2] = (keep[k] + got[k].astype(F32)).astype(out.dtype)

    def halve(keep, got, name):
        shape = (keep.shape[0] // 2,) + keep.shape[1:]
        return call(
            halve_kernel, [struct(shape, dtype) for dtype in (F32, BF)], [], name, keep, got
        )

    def left_kernel(z_ref, be_ref, keep, send, total):
        acc = None
        for a in range(4):
            b = be_ref[:, a].reshape(chan4 * cols, samples)
            d = dot_nn(jnp.transpose(b), z_ref[:, a].reshape(chan4 * cols, rows * chan))
            d = xor_groups(jnp.transpose(d), a, chan)
            acc = d if acc is None else acc + d
        total[...] = (acc * inv_samples).reshape(rows, chan, samples)
        hand_out_halves(total, keep, send, lax.axis_index("col"))

    left_keep, left_send = call(
        left_kernel,
        [struct((near, left_piece, chan, samples), dtype) for dtype in (F32, BF)],
        [pltpu.VMEM((rows, chan, samples), F32)],
        "left_grad",
        after(z, weight_send),
        right_e,
        cost=3,
    )

    for bit in bits_of(n_row)[:-1]:
        weight_got = after(swap(weight_send, "row", bit), left_send)
        weight_keep, weight_send = halve(weight_keep, weight_got, "weight_halve_%d" % bit)
    left_send = after(left_send, weight_send)

    def right_kernel(z_ref, *refs):
        a_refs, (keep, send, whole, total, turned) = refs[:n_col], refs[n_col:]
        assemble(whole, a_refs, 0, lax.axis_index("col"))
        am = whole[...].reshape(rows * chan, samples)
        for a in range(4):
            d = dot_nn(z_ref[:, a].reshape(chan4 * cols, rows * chan), xor_groups(am, a, chan))
            total[:, a] = d.reshape(chan4, cols, samples)
        turned[...] = jnp.swapaxes(total[...].reshape(chan, cols, samples), 0, 1) * inv_samples
        hand_out_halves(turned, keep, send, lax.axis_index("row"))

    right_keep, right_send = call(
        right_kernel,
        [struct((half, right_piece, chan, samples), dtype) for dtype in (F32, BF)],
        [
            pltpu.VMEM((rows, chan, samples), BF),
            pltpu.VMEM((chan4, 4, cols, samples), F32),
            pltpu.VMEM((cols, chan, samples), F32),
        ],
        "right_grad",
        after(z, weight_send),
        *left_parts,
        cost=3,
    )

    def last_kernel(keep, got, out):
        out[...] = (keep[0] + got[0].astype(F32)).astype(BF)

    (weight_own,) = call(
        last_kernel,
        [struct((weight_piece, width), BF)],
        [],
        "weight_row_sum",
        weight_keep,
        after(swap(weight_send, "row", half), right_send),
    )

    def pair_kernel(near_ref, far_ref, weight_ref, bias_ref, p_hbm, p_ref, sem):
        me = lax.axis_index("col")
        copies = []
        for part, y_ref in enumerate((near_ref, far_ref)):
            group = part ^ (me // near)
            for b in range(4):
                d = dot_nn(
                    y_ref[:, b].reshape(half4 * cols, pairs), xor_groups(weight_ref[...], b, chan)
                )
                d = d * inv_samples + bias_ref[...]
                p_ref[part, :, b] = d.reshape(half4, cols, width).astype(BF)
            copies.append(
                pltpu.make_async_copy(
                    p_ref.at[part], p_hbm.at[pl.ds(group * half4, half4)], sem.at[part]
                )
            )
            copies[-1].start()
        for copy in copies:
            copy.wait()

    (pair_update,) = call(
        pair_kernel,
        [struct((row4, 4, cols, width), BF)],
        [pltpu.VMEM((2, half4, 4, cols, width), BF), pltpu.SemaphoreType.DMA((2,))],
        "pair_update",
        after(y_near, weight_own),
        y_far,
        weight_e,
        out_bias.reshape(1, width),
        cost=16,
        hbm_out=(0,),
    )


    for bit in bits_of(n_row)[:-1]:
        right_got = after(swap(right_send, "row", bit), pair_update)
        right_keep, right_send = halve(right_keep, right_got, "right_halve_%d" % bit)
    right_got = swap(right_send, "row", half)


    def add_kernel(own, got, out):
        out[...] = (own[...].astype(F32) + got[...].astype(F32)).astype(BF)

    weight_sum, tied = weight_own, right_send
    for bit in reversed(bits_of(n_col)):
        weight_got = after(swap(weight_sum, "col", bit), tied)
        (weight_sum,) = call(
            add_kernel,
            [struct((weight_piece, width), BF)],
            [],
            "weight_col_sum_%d" % bit,
            weight_sum,
            weight_got,
        )
        if tied is right_send:
            for low in bits_of(n_col)[:-1]:
                left_got = after(swap(left_send, "col", low), weight_sum)
                left_keep, left_send = halve(left_keep, left_got, "left_halve_%d" % low)
            left_got = swap(left_send, "col", near)
            tied = left_send
    weight_rows = swap_all([weight_sum] * n_row, "row")

    def totals_kernel(l_keep, l_got, r_keep, r_got, *refs):
        l_out, r_out, w_out = refs[n_row:]
        l_out[...] = l_keep[...] + l_got[...].astype(F32)
        r_out[...] = r_keep[...] + r_got[...].astype(F32)
        me = lax.axis_index("row")
        for k in range(n_row):
            w_out[pl.ds((me ^ k) * weight_piece, weight_piece)] = refs[k][...].astype(F32)

    grad_left, grad_right, grad_weight = call(
        totals_kernel,
        [
            struct((1, left_piece, chan, samples), F32),
            struct((1, right_piece, chan, samples), F32),
            struct((pairs, width), F32),
        ],
        [],
        "totals",
        left_keep,
        left_got,
        right_keep,
        right_got,
        *weight_rows,
    )
    return (pair_update.reshape(rows, cols, width), grad_left, grad_right, grad_weight)


def solution(mesh):
    return jax.shard_map(
        on_device,
        mesh=mesh,
        in_specs=(
            P(("grp", "row"), "col", None, None),
            P(("grp", "col"), "row", None, None),
            P(),
            P(),
            P(("grp", "row"), "col", None),
        ),
        out_specs=(
            P(("grp", "row"), "col", None),
            P(("grp", "row"), "col", None, None),
            P(("grp", "col"), "row", None, None),
            P("grp", None),
        ),
        check_vma=False,
    )
```

```python
import jax
import jax.numpy as jnp
from jax import lax
from jax.experimental import pallas as pl
from jax.experimental.pallas import tpu as pltpu
from jax.sharding import PartitionSpec as P

BF = jnp.bfloat16
F32 = jnp.float32
VMEM = pl.BlockSpec(memory_space=pltpu.VMEM)
LANES = 128


def dot_nt(x, y):
    return lax.dot_general(x, y, (((1,), (1,)), ((), ())), preferred_element_type=F32)


def dot_tn(x, y):
    return lax.dot_general(x, y, (((0,), (0,)), ((), ())), preferred_element_type=F32)


def dot_nn(x, y):
    return lax.dot_general(x, y, (((1,), (0,)), ((), ())), preferred_element_type=F32)


def swap01(x):
    return jnp.swapaxes(x.astype(F32), 0, 1).astype(x.dtype)


def xor_groups(x, a, chan):
    n = x.shape[0] // (4 * chan)
    x4 = x.reshape(n, 4, chan, x.shape[-1])
    return jnp.concatenate([x4[:, p ^ a][:, None] for p in range(4)], axis=1).reshape(x.shape)


def lane_masks(rows, chan):
    group = lax.broadcasted_iota(jnp.int32, (rows, LANES), 1) // chan
    return (group % 2) == 1, (group // 2) == 1


def trade(xs, masks):
    low, high = masks
    u = [jnp.where(low, xs[a ^ 1], xs[a]) for a in range(4)]
    return [jnp.where(high, u[b ^ 2], u[b]) for b in range(4)]


def assemble(scratch, parts, first, me):
    piece = parts[0].shape[0]
    count = scratch.shape[0] // piece
    for k, part in enumerate(parts):
        scratch[pl.ds(((me ^ (first + k)) % count) * piece, piece)] = part[...]


def call(kernel, outs, scratch, name, *operands, cost=1, hbm_in=(), hbm_out=()):
    hbm = pl.BlockSpec(memory_space=pltpu.HBM)
    return pl.pallas_call(
        kernel,
        out_shape=outs,
        in_specs=[hbm if i in hbm_in else VMEM for i in range(len(operands))],
        out_specs=[hbm if i in hbm_out else VMEM for i in range(len(outs))],
        scratch_shapes=list(scratch),
        compiler_params=pltpu.CompilerParams(vmem_limit_bytes=24 * 1024 * 1024),
        cost_estimate=pl.CostEstimate(flops=cost * 2**30, bytes_accessed=2**16, transcendentals=0),
        name=name,
    )(*operands)


def hand_out_halves(total, keep, send, me):
    piece = keep.shape[1]
    for k in range(total.shape[0] // piece):
        out = send if k % 2 else keep
        out[k // 2] = total[pl.ds((me ^ k) * piece, piece)].astype(out.dtype)


def swap(x, axis, k):
    n = lax.axis_size(axis)
    return lax.ppermute(x, axis, [(d, d ^ k) for d in range(n)])


def swap_all(pieces, axis):
    return [pieces[0]] + [swap(pieces[k], axis, k) for k in range(1, len(pieces))]


def bits_of(n):
    return [1 << s for s in range(n.bit_length() - 1)]


def gather_halves(own, axis):
    n = lax.axis_size(axis)
    parts = {0: own}
    for bit in reversed(bits_of(n)):
        for k in sorted(parts):
            parts[k ^ bit] = swap(parts[k], axis, bit)
    return [parts[k] for k in range(n)]


def gather_far(own, axis):
    n = lax.axis_size(axis)
    return {0: own, n // 2: swap(own, axis, n // 2)}


def gather_rest(parts, axis):
    n = lax.axis_size(axis)
    for bit in reversed(bits_of(n)[:-1]):
        for k in sorted(parts):
            parts[k ^ bit] = swap(parts[k], axis, bit)
    return [parts[k] for k in range(n)]


def after(x, *earlier):
    return lax.optimization_barrier((x, earlier))[0]


def tree_sum(parts):
    parts = [part.astype(F32) for part in parts]
    while len(parts) > 1:
        parts = [parts[i] + parts[i + 1] for i in range(0, len(parts), 2)]
    return parts[0]


def on_device(left_factors, right_factors, out_weight, out_bias, pair_grad):
    n_row = lax.axis_size("row")
    n_col = lax.axis_size("col")
    left, right = left_factors[0], right_factors[0]
    left_piece, chan, samples = left.shape
    right_piece = right.shape[0]
    rows, cols, width = pair_grad.shape
    pairs = chan * chan
    row4, chan4 = rows // 4, chan // 4
    half4 = row4 // 2
    near, half = n_col // 2, n_row // 2
    inv_samples = 1.0 / samples
    wide = 2 * LANES
    weight_piece = pairs // n_row
    struct = jax.ShapeDtypeStruct
    weight3 = out_weight.reshape(chan, chan, width)
    grad4 = pair_grad.reshape(row4, 4, cols, width)

    left_parts = gather_far(left, "col")
    right_parts = swap_all([right] * n_row, "row")

    def tile(q, m, h):
        return q[m * cols : (m + 1) * cols, h * LANES : (h + 1) * LANES]

    def stage_kernel(grad_hbm, weight_hbm, left_hbm, right_hbm, grad, weight_e, left, right, *scr):
        weight, sems = scr
        copies = [
            pltpu.make_async_copy(source, target, sems.at[i])
            for i, (source, target) in enumerate(
                [(weight_hbm, weight), (left_hbm, left), (right_hbm, right), (grad_hbm, grad)]
            )
        ]
        for copy in copies:
            copy.start()
        copies[0].wait()
        weight_e[...] = swap01(weight[...]).reshape(pairs, width)
        for copy in copies[1:]:
            copy.wait()

    grad_vmem, weight_e, left_vmem, right_parts[0] = call(
        stage_kernel,
        [
            struct(grad4.shape, BF),
            struct((pairs, width), BF),
            struct(left.shape, BF),
            struct(right.shape, BF),
        ],
        [pltpu.VMEM(weight3.shape, BF), pltpu.SemaphoreType.DMA((4,))],
        "stage",
        *[pltpu.with_memory_space_constraint(x, pltpu.HBM) for x in (grad4, weight3, left, right)],
        hbm_in=(0, 1, 2, 3),
    )

    def outer_grad_kernel(grad_ref, weight_ref, z_ref):
        masks = lane_masks(cols, chan)
        ws = [xor_groups(weight_ref[...], b, chan) for b in range(4)]
        for blk in range(pairs // wide):
            for n in range(0, row4, 4):
                qs = [
                    dot_nt(
                        grad_ref[n : n + 4, b].reshape(4 * cols, width),
                        ws[b][blk * wide : (blk + 1) * wide],
                    ).astype(BF)
                    for b in range(4)
                ]
                for m, h in [(m, h) for m in range(4) for h in range(2)]:
                    ys = trade([tile(q, m, h) for q in qs], masks)
                    for a in range(4):
                        z_ref[2 * blk + h, a, :, (n + m) * LANES : (n + m + 1) * LANES] = ys[a]

    (z,) = call(
        outer_grad_kernel,
        [struct((chan4, 4, cols, rows * chan), BF)],
        [],
        "outer_grad",
        grad_vmem,
        weight_e,
        cost=0,
    )

    left_parts[near] = after(left_parts[near], z)
    left_parts = gather_rest(left_parts, "col")
    left_parts[0] = left_vmem

    def outer_mean(a_whole, be, grad_ref, y_ref, group, masks):
        am = a_whole[...].reshape(rows * chan // 2, samples)
        ams = [xor_groups(am, a, chan) for a in range(4)]
        for blk in range(rows * chan // 2 // wide):
            for e in range(0, chan4, 4):
                qs = [
                    dot_nt(
                        be[e : e + 4, a].reshape(4 * cols, samples),
                        ams[a][blk * wide : (blk + 1) * wide],
                    ).astype(BF)
                    for a in range(4)
                ]
                for m, h in [(m, h) for m in range(4) for h in range(2)]:
                    ys = trade([tile(q, m, h) for q in qs], masks)
                    for b in range(4):
                        y_ref[2 * blk + h, b, :, (e + m) * LANES : (e + m + 1) * LANES] = ys[b]
        acc = None
        for b in range(4):
            g = grad_ref[pl.ds(group * half4, half4), b].reshape(half4 * cols, width)
            d = dot_nn(jnp.transpose(g), y_ref[:, b].reshape(half4 * cols, pairs))
            d = xor_groups(jnp.transpose(d), b, chan)
            acc = d if acc is None else acc + d
        return acc

    mean_scratch = [pltpu.VMEM((rows // 2, chan, samples), BF)]

    def near_kernel(grad_ref, *refs):
        a_refs, b_refs = refs[:near], refs[near : near + n_row]
        y_ref, weight_ref, be_ref, a_whole, b_whole = refs[near + n_row :]
        me = lax.axis_index("col")
        assemble(a_whole, a_refs, 0, me)
        assemble(b_whole, b_refs, 0, lax.axis_index("row"))
        be = swap01(b_whole[...]).reshape(chan4, 4, cols, samples)
        be_ref[...] = be
        weight_ref[...] = outer_mean(
            a_whole, be, grad_ref, y_ref, me // near, lane_masks(cols, chan)
        )

    y_struct = struct((half4, 4, cols, pairs), BF)
    y_near, weight_near, right_e = call(
        near_kernel,
        [y_struct, struct((pairs, width), F32), struct((chan4, 4, cols, samples), BF)],
        mean_scratch + [pltpu.VMEM((cols, chan, samples), BF)],
        "outer_mean_near",
        grad_vmem,
        *left_parts[:near],
        *right_parts,
    )

    def far_kernel(grad_ref, be_ref, near_ref, *refs):
        a_refs, y_ref = refs[:near], refs[near]
        keep, send, a_whole, total = refs[near + 1 :]
        me = lax.axis_index("col")
        assemble(a_whole, a_refs, near, me)
        acc = outer_mean(
            a_whole, be_ref, grad_ref, y_ref, 1 - me // near, lane_masks(cols, chan)
        )
        acc = (acc + near_ref[...]) * (inv_samples / (rows * n_row))
        total[...] = jnp.swapaxes(acc.reshape(chan, chan, width), 0, 1).reshape(pairs, width)
        hand_out_halves(total, keep, send, lax.axis_index("row"))

    y_far, weight_keep, weight_send = call(
        far_kernel,
        [y_struct] + [struct((half, weight_piece, width), F32)] * 2,
        mean_scratch + [pltpu.VMEM((pairs, width), F32)],
        "outer_mean_far",
        grad_vmem,
        right_e,
        weight_near,
        *left_parts[near:],
    )
    def halve_kernel(keep, got, next_keep, next_send):
        for k in range(keep.shape[0]):
            out = next_send if k % 2 else next_keep
            out[k // 2] = (keep[k] + got[k].astype(F32)).astype(out.dtype)

    def halve(keep, got, name):
        shape = (keep.shape[0] // 2,) + keep.shape[1:]
        return call(
            halve_kernel, [struct(shape, dtype) for dtype in (F32, BF)], [], name, keep, got
        )

    def left_kernel(z_ref, be_ref, keep, send, total):
        acc = None
        for a in range(4):
            b = be_ref[:, a].reshape(chan4 * cols, samples)
            d = dot_nn(jnp.transpose(b), z_ref[:, a].reshape(chan4 * cols, rows * chan))
            d = xor_groups(jnp.transpose(d), a, chan)
            acc = d if acc is None else acc + d
        total[...] = (acc * inv_samples).reshape(rows, chan, samples)
        hand_out_halves(total, keep, send, lax.axis_index("col"))

    left_keep, left_send = call(
        left_kernel,
        [struct((near, left_piece, chan, samples), dtype) for dtype in (F32, BF)],
        [pltpu.VMEM((rows, chan, samples), F32)],
        "left_grad",
        after(z, weight_send),
        right_e,
        cost=3,
    )

    for bit in bits_of(n_row)[:-1]:
        weight_got = after(swap(weight_send, "row", bit), left_send)
        weight_keep, weight_send = halve(weight_keep, weight_got, "weight_halve_%d" % bit)

    def right_kernel(z_ref, *refs):
        a_refs, (keep, send, whole, total, turned) = refs[:n_col], refs[n_col:]
        assemble(whole, a_refs, 0, lax.axis_index("col"))
        am = whole[...].reshape(rows * chan, samples)
        for a in range(4):
            d = dot_nn(z_ref[:, a].reshape(chan4 * cols, rows * chan), xor_groups(am, a, chan))
            total[:, a] = d.reshape(chan4, cols, samples)
        turned[...] = jnp.swapaxes(total[...].reshape(chan, cols, samples), 0, 1) * inv_samples
        hand_out_halves(turned, keep, send, lax.axis_index("row"))

    right_keep, right_send = call(
        right_kernel,
        [struct((half, right_piece, chan, samples), dtype) for dtype in (F32, BF)],
        [
            pltpu.VMEM((rows, chan, samples), BF),
            pltpu.VMEM((chan4, 4, cols, samples), F32),
            pltpu.VMEM((cols, chan, samples), F32),
        ],
        "right_grad",
        after(z, weight_send),
        *left_parts,
        cost=3,
    )

    def last_kernel(keep, got, out):
        out[...] = (keep[0] + got[0].astype(F32)).astype(BF)

    (weight_own,) = call(
        last_kernel,
        [struct((weight_piece, width), BF)],
        [],
        "weight_row_sum",
        weight_keep,
        after(swap(weight_send, "row", half), right_send),
    )

    def pair_kernel(near_ref, far_ref, weight_ref, bias_ref, p_hbm, p_ref, sem):
        me = lax.axis_index("col")
        copies = []
        for part, y_ref in enumerate((near_ref, far_ref)):
            group = part ^ (me // near)
            for b in range(4):
                d = dot_nn(
                    y_ref[:, b].reshape(half4 * cols, pairs), xor_groups(weight_ref[...], b, chan)
                )
                d = d * inv_samples + bias_ref[...]
                p_ref[part, :, b] = d.reshape(half4, cols, width).astype(BF)
            copies.append(
                pltpu.make_async_copy(
                    p_ref.at[part], p_hbm.at[pl.ds(group * half4, half4)], sem.at[part]
                )
            )
            copies[-1].start()
        for copy in copies:
            copy.wait()

    (pair_update,) = call(
        pair_kernel,
        [struct((row4, 4, cols, width), BF)],
        [pltpu.VMEM((2, half4, 4, cols, width), BF), pltpu.SemaphoreType.DMA((2,))],
        "pair_update",
        after(y_near, weight_own),
        y_far,
        weight_e,
        out_bias.reshape(1, width),
        cost=16,
        hbm_out=(0,),
    )


    for bit in bits_of(n_row)[:-1]:
        right_got = after(swap(right_send, "row", bit), pair_update)
        right_keep, right_send = halve(right_keep, right_got, "right_halve_%d" % bit)
    right_got = swap(right_send, "row", half)


    def add_kernel(own, got, out):
        out[...] = (own[...].astype(F32) + got[...].astype(F32)).astype(BF)

    weight_sum, tied = weight_own, right_send
    for bit in reversed(bits_of(n_col)):
        weight_got = after(swap(weight_sum, "col", bit), tied)
        (weight_sum,) = call(
            add_kernel,
            [struct((weight_piece, width), BF)],
            [],
            "weight_col_sum_%d" % bit,
            weight_sum,
            weight_got,
        )
        if tied is right_send:
            for low in bits_of(n_col)[:-1]:
                left_got = after(swap(left_send, "col", low), weight_sum)
                left_keep, left_send = halve(left_keep, left_got, "left_halve_%d" % low)
            left_got = swap(left_send, "col", near)
            tied = left_send
    weight_rows = swap_all([weight_sum] * n_row, "row")

    def totals_kernel(l_keep, l_got, r_keep, r_got, *refs):
        l_out, r_out, w_out = refs[n_row:]
        l_out[...] = l_keep[...] + l_got[...].astype(F32)
        r_out[...] = r_keep[...] + r_got[...].astype(F32)
        me = lax.axis_index("row")
        for k in range(n_row):
            w_out[pl.ds((me ^ k) * weight_piece, weight_piece)] = refs[k][...].astype(F32)

    grad_left, grad_right, grad_weight = call(
        totals_kernel,
        [
            struct((1, left_piece, chan, samples), F32),
            struct((1, right_piece, chan, samples), F32),
            struct((pairs, width), F32),
        ],
        [],
        "totals",
        left_keep,
        left_got,
        right_keep,
        right_got,
        *weight_rows,
    )
    return (pair_update.reshape(rows, cols, width), grad_left, grad_right, grad_weight)


def solution(mesh):
    return jax.shard_map(
        on_device,
        mesh=mesh,
        in_specs=(
            P(("grp", "row"), "col", None, None),
            P(("grp", "col"), "row", None, None),
            P(),
            P(),
            P(("grp", "row"), "col", None),
        ),
        out_specs=(
            P(("grp", "row"), "col", None),
            P(("grp", "row"), "col", None, None),
            P(("grp", "col"), "row", None, None),
            P("grp", None),
        ),
        check_vma=False,
    )
```

```python
import jax
import jax.numpy as jnp
from jax import lax
from jax.experimental import pallas as pl
from jax.experimental.pallas import tpu as pltpu
from jax.sharding import PartitionSpec as P

BF = jnp.bfloat16
F32 = jnp.float32
VMEM = pl.BlockSpec(memory_space=pltpu.VMEM)
LANES = 128


def dot_nt(x, y):
    return lax.dot_general(x, y, (((1,), (1,)), ((), ())), preferred_element_type=F32)


def dot_nn(x, y):
    return lax.dot_general(x, y, (((1,), (0,)), ((), ())), preferred_element_type=F32)


def swap01(x):
    return jnp.swapaxes(x.astype(F32), 0, 1).astype(x.dtype)


def xor_groups(x, a, chan):
    n = x.shape[0] // (4 * chan)
    x4 = x.reshape(n, 4, chan, x.shape[-1])
    return jnp.concatenate([x4[:, p ^ a][:, None] for p in range(4)], axis=1).reshape(x.shape)


def lane_masks(rows, chan):
    group = lax.broadcasted_iota(jnp.int32, (rows, LANES), 1) // chan
    return (group % 2) == 1, (group // 2) == 1


def trade(xs, masks):
    low, high = masks
    u = [jnp.where(low, xs[a ^ 1], xs[a]) for a in range(4)]
    return [jnp.where(high, u[b ^ 2], u[b]) for b in range(4)]


def assemble(scratch, parts, first, me):
    piece = parts[0].shape[0]
    count = scratch.shape[0] // piece
    for k, part in enumerate(parts):
        scratch[pl.ds(((me ^ (first + k)) % count) * piece, piece)] = part[...]


def call(kernel, outs, scratch, name, *operands, cost=1, hbm_in=(), hbm_out=()):
    hbm = pl.BlockSpec(memory_space=pltpu.HBM)
    return pl.pallas_call(
        kernel,
        out_shape=outs,
        in_specs=[hbm if i in hbm_in else VMEM for i in range(len(operands))],
        out_specs=[hbm if i in hbm_out else VMEM for i in range(len(outs))],
        scratch_shapes=list(scratch),
        compiler_params=pltpu.CompilerParams(vmem_limit_bytes=24 * 1024 * 1024),
        cost_estimate=pl.CostEstimate(flops=cost * 2**30, bytes_accessed=2**16, transcendentals=0),
        name=name,
    )(*operands)


def hand_out_halves(total, keep, send, me):
    piece = keep.shape[1]
    for k in range(total.shape[0] // piece):
        out = send if k % 2 else keep
        out[k // 2] = total[pl.ds((me ^ k) * piece, piece)].astype(out.dtype)


def swap(x, axis, k):
    n = lax.axis_size(axis)
    return lax.ppermute(x, axis, [(d, d ^ k) for d in range(n)])


def swap_all(pieces, axis):
    return [pieces[0]] + [swap(pieces[k], axis, k) for k in range(1, len(pieces))]


def bits_of(n):
    return [1 << s for s in range(n.bit_length() - 1)]


def gather_far(own, axis):
    n = lax.axis_size(axis)
    return {0: own, n // 2: swap(own, axis, n // 2)}


def gather_rest(parts, axis):
    n = lax.axis_size(axis)
    for bit in reversed(bits_of(n)[:-1]):
        for k in sorted(parts):
            parts[k ^ bit] = swap(parts[k], axis, bit)
    return [parts[k] for k in range(n)]


def after(x, *earlier):
    return lax.optimization_barrier((x, earlier))[0]


def on_device(left_factors, right_factors, out_weight, out_bias, pair_grad):
    n_row = lax.axis_size("row")
    n_col = lax.axis_size("col")
    left, right = left_factors[0], right_factors[0]
    left_piece, chan, samples = left.shape
    right_piece = right.shape[0]
    rows, cols, width = pair_grad.shape
    pairs = chan * chan
    row4, chan4 = rows // 4, chan // 4
    near, half = n_col // 2, n_row // 2
    inv_samples = 1.0 / samples
    wide = 2 * LANES
    weight_piece = pairs // n_row
    struct = jax.ShapeDtypeStruct
    weight3 = out_weight.reshape(chan, chan, width)
    grad4 = pair_grad.reshape(row4, 4, cols, width)

    left_parts = gather_far(left, "col")
    right_parts = swap_all([right] * n_row, "row")

    def tile(q, m, h):
        return q[m * cols : (m + 1) * cols, h * LANES : (h + 1) * LANES]

    def stage_kernel(grad_hbm, weight_hbm, left_hbm, right_hbm, grad, weight_e, left, right, *scr):
        weight, sems = scr
        copies = [
            pltpu.make_async_copy(source, target, sems.at[i])
            for i, (source, target) in enumerate(
                [(weight_hbm, weight), (left_hbm, left), (right_hbm, right), (grad_hbm, grad)]
            )
        ]
        for copy in copies:
            copy.start()
        copies[0].wait()
        weight_e[...] = swap01(weight[...]).reshape(pairs, width)
        for copy in copies[1:]:
            copy.wait()

    grad_vmem, weight_e, left_vmem, right_parts[0] = call(
        stage_kernel,
        [
            struct(grad4.shape, BF),
            struct((pairs, width), BF),
            struct(left.shape, BF),
            struct(right.shape, BF),
        ],
        [pltpu.VMEM(weight3.shape, BF), pltpu.SemaphoreType.DMA((4,))],
        "stage",
        *[pltpu.with_memory_space_constraint(x, pltpu.HBM) for x in (grad4, weight3, left, right)],
        hbm_in=(0, 1, 2, 3),
    )

    def outer_grad_kernel(grad_ref, weight_ref, z_ref):
        masks = lane_masks(cols, chan)
        ws = [xor_groups(weight_ref[...], b, chan) for b in range(4)]
        for blk in range(pairs // wide):
            for n in range(0, row4, 4):
                qs = [
                    dot_nt(
                        grad_ref[n : n + 4, b].reshape(4 * cols, width),
                        ws[b][blk * wide : (blk + 1) * wide],
                    ).astype(BF)
                    for b in range(4)
                ]
                for m, h in [(m, h) for m in range(4) for h in range(2)]:
                    ys = trade([tile(q, m, h) for q in qs], masks)
                    for a in range(4):
                        z_ref[2 * blk + h, a, :, (n + m) * LANES : (n + m + 1) * LANES] = ys[a]

    (z,) = call(
        outer_grad_kernel,
        [struct((chan4, 4, cols, rows * chan), BF)],
        [],
        "outer_grad",
        grad_vmem,
        weight_e,
        cost=0,
    )

    left_parts[near] = after(left_parts[near], z)
    left_parts = gather_rest(left_parts, "col")
    left_parts[0] = left_vmem

    def outer_mean(a_refs, first, be, grad_ref, y_ref, a_whole):
        me = lax.axis_index("col")
        count = a_whole.shape[0]
        assemble(a_whole, a_refs, first, me)
        group = (me ^ first) // len(a_refs)
        masks = lane_masks(cols, chan)
        ams = [xor_groups(a_whole[...].reshape(count * chan, samples), a, chan) for a in range(4)]
        for at in range(0, count * chan, wide):
            size = min(wide, count * chan - at)
            for e in range(0, chan4, 4):
                qs = [
                    dot_nt(be[e : e + 4, a].reshape(4 * cols, samples), ams[a][at : at + size])
                    for a in range(4)
                ]
                qs = [q.astype(BF) for q in qs]
                for m, h in [(m, h) for m in range(4) for h in range(size // LANES)]:
                    ys = trade([tile(q, m, h) for q in qs], masks)
                    for b in range(4):
                        lanes = slice((e + m) * LANES, (e + m + 1) * LANES)
                        y_ref[at // LANES + h, b, :, lanes] = ys[b]
        acc = None
        for b in range(4):
            g = grad_ref[pl.ds(group * (count // 4), count // 4), b]
            d = dot_nn(
                jnp.transpose(g.reshape(count // 4 * cols, width)),
                y_ref[:, b].reshape(count // 4 * cols, pairs),
            )
            d = xor_groups(jnp.transpose(d), b, chan)
            acc = d if acc is None else acc + d
        return acc

    bounds = [0, near, near + near // 2, n_col]

    def mean_outs(step):
        count = (bounds[step + 1] - bounds[step]) * left_piece
        y = struct((count // 4, 4, cols, pairs), BF)
        return y, pltpu.VMEM((count, chan, samples), BF)

    def near_kernel(grad_ref, *refs):
        a_refs, b_refs = refs[:near], refs[near : near + n_row]
        y_ref, acc_ref, be_ref, a_whole, b_whole = refs[near + n_row :]
        assemble(b_whole, b_refs, 0, lax.axis_index("row"))
        be_ref[...] = swap01(b_whole[...]).reshape(chan4, 4, cols, samples)
        acc_ref[...] = outer_mean(a_refs, 0, be_ref, grad_ref, y_ref, a_whole)

    y_struct, whole = mean_outs(0)
    y_near, weight_near, right_e = call(
        near_kernel,
        [y_struct, struct((pairs, width), F32), struct((chan4, 4, cols, samples), BF)],
        [whole, pltpu.VMEM((cols, chan, samples), BF)],
        "outer_mean_near",
        after(grad_vmem, z),
        *left_parts[:near],
        *right_parts,
    )

    def middle_kernel(grad_ref, be_ref, before_ref, *refs):
        a_refs, (y_ref, acc_ref, a_whole) = refs[:-3], refs[-3:]
        acc = outer_mean(a_refs, bounds[1], be_ref, grad_ref, y_ref, a_whole)
        acc_ref[...] = acc + before_ref[...]

    y_struct, whole = mean_outs(1)
    y_middle, weight_middle = call(
        middle_kernel,
        [y_struct, struct((pairs, width), F32)],
        [whole],
        "outer_mean_middle",
        grad_vmem,
        right_e,
        weight_near,
        *left_parts[bounds[1] : bounds[2]],
    )

    def far_kernel(grad_ref, be_ref, before_ref, *refs):
        a_refs, (y_ref, keep, send, a_whole, total) = refs[:-5], refs[-5:]
        acc = outer_mean(a_refs, bounds[2], be_ref, grad_ref, y_ref, a_whole)
        acc = (acc + before_ref[...]) * (inv_samples / (rows * n_row))
        total[...] = jnp.swapaxes(acc.reshape(chan, chan, width), 0, 1).reshape(pairs, width)
        hand_out_halves(total, keep, send, lax.axis_index("row"))

    y_struct, whole = mean_outs(2)
    y_far, weight_keep, weight_send = call(
        far_kernel,
        [y_struct] + [struct((half, weight_piece, width), F32)] * 2,
        [whole, pltpu.VMEM((pairs, width), F32)],
        "outer_mean_far",
        grad_vmem,
        right_e,
        weight_middle,
        *left_parts[bounds[2] :],
    )

    def halve_kernel(keep, got, next_keep, next_send):
        for k in range(keep.shape[0]):
            out = next_send if k % 2 else next_keep
            out[k // 2] = (keep[k] + got[k].astype(F32)).astype(out.dtype)

    def halve(keep, got, name):
        shape = (keep.shape[0] // 2,) + keep.shape[1:]
        return call(
            halve_kernel, [struct(shape, dtype) for dtype in (F32, BF)], [], name, keep, got
        )

    def left_kernel(z_ref, be_ref, keep, send, total):
        acc = None
        for a in range(4):
            b = be_ref[:, a].reshape(chan4 * cols, samples)
            d = dot_nn(jnp.transpose(b), z_ref[:, a].reshape(chan4 * cols, rows * chan))
            d = xor_groups(jnp.transpose(d), a, chan)
            acc = d if acc is None else acc + d
        total[...] = (acc * inv_samples).reshape(rows, chan, samples)
        hand_out_halves(total, keep, send, lax.axis_index("col"))

    left_keep, left_send = call(
        left_kernel,
        [struct((near, left_piece, chan, samples), dtype) for dtype in (F32, BF)],
        [pltpu.VMEM((rows, chan, samples), F32)],
        "left_grad",
        after(z, weight_send),
        right_e,
        cost=3,
    )

    for bit in bits_of(n_row)[:-1]:
        weight_got = after(swap(weight_send, "row", bit), left_send)
        weight_keep, weight_send = halve(weight_keep, weight_got, "weight_halve_%d" % bit)

    def right_kernel(z_ref, *refs):
        a_refs, (keep, send, whole, total, turned) = refs[:n_col], refs[n_col:]
        assemble(whole, a_refs, 0, lax.axis_index("col"))
        am = whole[...].reshape(rows * chan, samples)
        for a in range(4):
            d = dot_nn(z_ref[:, a].reshape(chan4 * cols, rows * chan), xor_groups(am, a, chan))
            total[:, a] = d.reshape(chan4, cols, samples)
        turned[...] = jnp.swapaxes(total[...].reshape(chan, cols, samples), 0, 1) * inv_samples
        hand_out_halves(turned, keep, send, lax.axis_index("row"))

    right_keep, right_send = call(
        right_kernel,
        [struct((half, right_piece, chan, samples), dtype) for dtype in (F32, BF)],
        [
            pltpu.VMEM((rows, chan, samples), BF),
            pltpu.VMEM((chan4, 4, cols, samples), F32),
            pltpu.VMEM((cols, chan, samples), F32),
        ],
        "right_grad",
        after(z, weight_send),
        *left_parts,
        cost=3,
    )

    def last_kernel(keep, got, out):
        out[...] = (keep[0] + got[0].astype(F32)).astype(BF)

    (weight_own,) = call(
        last_kernel,
        [struct((weight_piece, width), BF)],
        [],
        "weight_row_sum",
        weight_keep,
        after(swap(weight_send, "row", half), right_send),
    )

    ys = [y_near, y_middle, y_far]

    def pair_kernel(*refs):
        y_refs, (weight_ref, bias_ref, p_hbm, p_ref, sem) = refs[:3], refs[3:]
        me = lax.axis_index("col")
        copies = []
        at = 0
        for step, y_ref in enumerate(y_refs):
            count = y_ref.shape[0]
            group = (me ^ bounds[step]) // (bounds[step + 1] - bounds[step])
            for b in range(4):
                d = dot_nn(
                    y_ref[:, b].reshape(count * cols, pairs), xor_groups(weight_ref[...], b, chan)
                )
                d = d * inv_samples + bias_ref[...]
                p_ref[at : at + count, b] = d.reshape(count, cols, width).astype(BF)
            copies.append(
                pltpu.make_async_copy(
                    p_ref.at[pl.ds(at, count)], p_hbm.at[pl.ds(group * count, count)], sem.at[step]
                )
            )
            copies[-1].start()
            at += count
        for copy in copies:
            copy.wait()

    (pair_update,) = call(
        pair_kernel,
        [struct((row4, 4, cols, width), BF)],
        [pltpu.VMEM((row4, 4, cols, width), BF), pltpu.SemaphoreType.DMA((3,))],
        "pair_update",
        after(ys[0], weight_own),
        *ys[1:],
        weight_e,
        out_bias.reshape(1, width),
        cost=16,
        hbm_out=(0,),
    )


    for bit in bits_of(n_row)[:-1]:
        right_got = after(swap(right_send, "row", bit), pair_update)
        right_keep, right_send = halve(right_keep, right_got, "right_halve_%d" % bit)
    right_got = swap(right_send, "row", half)


    def add_kernel(own, got, out):
        out[...] = (own[...].astype(F32) + got[...].astype(F32)).astype(BF)

    weight_sum, tied = weight_own, right_send
    for bit in reversed(bits_of(n_col)):
        weight_got = after(swap(weight_sum, "col", bit), tied)
        (weight_sum,) = call(
            add_kernel,
            [struct((weight_piece, width), BF)],
            [],
            "weight_col_sum_%d" % bit,
            weight_sum,
            weight_got,
        )
        if tied is right_send:
            for low in bits_of(n_col)[:-1]:
                left_got = after(swap(left_send, "col", low), weight_sum)
                left_keep, left_send = halve(left_keep, left_got, "left_halve_%d" % low)
            left_got = swap(left_send, "col", near)
            tied = left_send
    weight_rows = swap_all([weight_sum] * n_row, "row")

    def totals_kernel(l_keep, l_got, r_keep, r_got, l_out, r_out):
        l_out[...] = l_keep[...] + l_got[...].astype(F32)
        r_out[...] = r_keep[...] + r_got[...].astype(F32)

    grad_left, grad_right = call(
        totals_kernel,
        [
            struct((1, left_piece, chan, samples), F32),
            struct((1, right_piece, chan, samples), F32),
        ],
        [],
        "left_right_totals",
        after(left_keep, weight_sum),
        left_got,
        right_keep,
        right_got,
    )

    def place_kernel(*refs):
        w_hbm, wide_ref, sems = refs[n_row:]
        me = lax.axis_index("row")
        copies = []
        for k in range(n_row):
            wide_ref[k] = refs[k][...].astype(F32)
            target = w_hbm.at[pl.ds((me ^ k) * weight_piece, weight_piece)]
            copies.append(pltpu.make_async_copy(wide_ref.at[k], target, sems.at[k]))
            copies[-1].start()
        for copy in copies:
            copy.wait()

    weight_rows[-1] = after(weight_rows[-1], grad_right)
    (grad_weight,) = call(
        place_kernel,
        [struct((pairs, width), F32)],
        [
            pltpu.VMEM((n_row, weight_piece, width), F32),
            pltpu.SemaphoreType.DMA((n_row,)),
        ],
        "weight_place",
        *weight_rows,
        hbm_out=(0,),
    )
    return (pair_update.reshape(rows, cols, width), grad_left, grad_right, grad_weight)


def solution(mesh):
    return jax.shard_map(
        on_device,
        mesh=mesh,
        in_specs=(
            P(("grp", "row"), "col", None, None),
            P(("grp", "col"), "row", None, None),
            P(),
            P(),
            P(("grp", "row"), "col", None),
        ),
        out_specs=(
            P(("grp", "row"), "col", None),
            P(("grp", "row"), "col", None, None),
            P(("grp", "col"), "row", None, None),
            P("grp", None),
        ),
        check_vma=False,
    )
```
